256 devices in a mesh: mp: 16 (over y, z_lo), fsdp: 16 (over z_hi, x, core).
Axes of the slice: x: 4, y: 4, z: 8 (z_hi: 2, z_lo: 4; z = z_hi * 4 + z_lo), core: 2. Of those that a mesh axis runs over, the one named last changes fastest.
Arguments:
- hidden: bfloat16 [16, 256, 16, 2048], P('mp', 'fsdp'), may hold values from -6 to 6
- gain: float32 [16, 2048], P('mp'), may hold values from 0.25 to 1.75
- head: bfloat16 [16, 2048, 36864], P('mp', None, 'fsdp'), may hold values from -0.125 to 0.125
- partner: int32 [16], replicated, may hold values from 0 to 15, as said below
- codes: int32 [256, 16], replicated, may hold values from 0 to 36863
Outputs:
- grad_hidden: bfloat16 [16, 256, 16, 2048], P('mp', 'fsdp')
- note_loss: float32 [16, 256], P('mp', 'fsdp')
- grad_gain: float32 [16, 2048], P('mp')
The draws below stay inside these ranges and needn't reach their ends.
Inputs may be any that keep to these rules, and one draw needn't show every extreme that they name: partner[partner[m]] == m and partner[m] != m for every model m. `codes`: a note may list a label number more than once.
All inputs are finite; a program needn't handle non-finite values.
Results may differ from the reference program's by a relative error of at most 0.0051.
Values may be sent and summed in bfloat16 or wider, within the bound.
A program may use at most 128 MiB of HBM per device.

```python
import math
import jax
import jax.numpy as jnp
import numpy as np
from jax import lax

D = 2048
SEQ = 16
CODES = 16
MODELS = 16
NOTES = 256
LABELS = 36864


def draw_partner(key, part):
    key = jax.random.fold_in(key, 7)
    order_key, pick_key = jax.random.split(key)
    half_count = MODELS // 2
    shuffled = jax.random.permutation(order_key, MODELS).astype(jnp.int32)
    ranking = jnp.argsort(shuffled, stable=True).astype(jnp.int32)
    chosen = jax.random.randint(pick_key, (), 0, half_count, dtype=jnp.int32)
    model_ids = jnp.arange(MODELS, dtype=jnp.int32)
    priority = jnp.where(model_ids == chosen, jnp.int32(-4), jnp.where(model_ids == chosen + half_count, jnp.int32(-3), jnp.where(model_ids == chosen + 1, jnp.int32(-2), jnp.where(model_ids == chosen + 2, jnp.int32(-1), ranking))))
    ordering = jnp.argsort(priority, stable=True).astype(jnp.int32)
    position = jnp.argsort(ordering, stable=True).astype(jnp.int32)
    return ordering[jnp.bitwise_xor(position, 1)]


def with_ends(array, key, least, top_value):
    index_at = [jax.random.randint(jax.random.fold_in(key, axis), (), 0, length) for axis, length in enumerate(array.shape)]
    widest = array.shape.index(max(array.shape))
    beside = index_at[:widest] + [(index_at[widest] + 1) % array.shape[widest]] + index_at[widest + 1:]
    return array.at[tuple(index_at)].set(least).at[tuple(beside)].set(top_value)


def levels(own_key, shape, pieces, low, largest):
    level, own = 1.0, jax.random.fold_in(own_key, 6)
    for dim, shards_of in pieces:
        steps = jnp.exp(jax.random.uniform(jax.random.fold_in(own, dim), (shards_of,), jnp.float32, low / len(pieces), largest / len(pieces)))
        level = level * jnp.repeat(steps, shape[dim] // shards_of).reshape([-1 if axis == dim else 1 for axis in range(len(shape))])
    return level


def rank_table(amount, slope):
    portions = [(1 << 20) // math.isqrt(standing ** slope) + 1 for standing in range(1, amount + 1)]
    width = 1 + sum(portions) // (1 << 30)
    return np.cumsum(np.array([max(1, weight // width) for weight in portions]))


def ranked_ids(rng, extent, number_of, skew):
    grid = rank_table(number_of, skew)
    pick = jax.random.randint(jax.random.fold_in(rng, 1), extent, 0, int(grid[number_of - 1]))
    rank = jnp.searchsorted(jnp.asarray(grid, jnp.int32), pick, side="right")
    return jax.random.permutation(jax.random.fold_in(rng, 2), number_of)[rank].astype(jnp.int32)


def noise(own_key, dims, width, limit, shards=(), held_as=jnp.bfloat16):
    values = width * jax.random.normal(own_key, dims, jnp.float32)
    if shards:
        values = values * levels(own_key, dims, shards, -0.22, 0.18)
    return jnp.clip(values, -limit, limit).astype(held_as)


def setup_inputs(seed: int = 0) -> dict:
    key_list = jax.random.split(jax.random.key(seed), 6)
    return {
        "hidden": noise(key_list[0], (MODELS, NOTES, SEQ, D), 1.0, 6.0, ((0, 16), (1, 16))),
        "gain": jnp.clip(1.0 + 0.15 * jax.random.normal(key_list[1], (MODELS, D), jnp.float32), 0.25, 1.75),
        "head": noise(key_list[2], (MODELS, D, LABELS), D ** -0.5, 0.125, ((0, 16), (2, 16))),
        "partner": draw_partner(jax.random.fold_in(key_list[5], 71), 0),
        "codes": with_ends(ranked_ids(key_list[4], (NOTES, CODES), LABELS, 2), jax.random.fold_in(key_list[4], 3), 0, LABELS - 1).astype(jnp.int32),
    }


epsilon = 1e-05
smoothing_heat_scale = 2.0
mentor_penalty_factor = 0.5

def normalize(hidden_rows):
    states = hidden_rows.astype(jnp.float32)
    inverse_rms = lax.rsqrt(lax.optimization_barrier(jnp.mean(states * states, axis=-1, keepdims=True)) + epsilon)
    return (states * inverse_rms, inverse_rms)

def reference(hidden, gain, head, partner, codes):
    pool_scale = 1.0 / math.sqrt(SEQ)

    def forward(inputs):
        hidden_rows, gains, weights = inputs
        normed, inverse_rms = normalize(hidden_rows)
        pooled = (lax.optimization_barrier(jnp.sum(normed, axis=1)) * gains * pool_scale).astype(jnp.bfloat16)
        return jnp.dot(pooled, weights, preferred_element_type=jnp.float32).astype(jnp.bfloat16)
    logits = lax.map(forward, (hidden, gain, head))
    note_index = jnp.arange(NOTES, dtype=jnp.int32)[:, None]
    diagnosis_truth = jnp.zeros((NOTES, LABELS), jnp.float32).at[note_index, codes].set(1.0)

    def backward(inputs):
        hidden_rows, gains, weights, partner_id, model_id = inputs
        learner_score_matrix = lax.dynamic_index_in_dim(logits, model_id, 0, keepdims=False).astype(jnp.float32)
        peer_score_matrix = lax.dynamic_index_in_dim(logits, partner_id, 0, keepdims=False).astype(jnp.float32)
        smoothed_diagnosis_truth = jax.nn.sigmoid(peer_score_matrix / smoothing_heat_scale)
        combined_cost_sum = jax.nn.softplus(learner_score_matrix) - diagnosis_truth * learner_score_matrix + mentor_penalty_factor * smoothing_heat_scale * smoothing_heat_scale * (jax.nn.softplus(learner_score_matrix / smoothing_heat_scale) - smoothed_diagnosis_truth * learner_score_matrix / smoothing_heat_scale)
        note_loss = lax.optimization_barrier(jnp.sum(combined_cost_sum, axis=1)) / LABELS
        score_derivative = (jax.nn.sigmoid(learner_score_matrix) - diagnosis_truth + mentor_penalty_factor * smoothing_heat_scale * (jax.nn.sigmoid(learner_score_matrix / smoothing_heat_scale) - smoothed_diagnosis_truth)).astype(jnp.bfloat16)
        dpooled = jnp.dot(score_derivative, weights.T, preferred_element_type=jnp.float32)
        normed, inverse_rms = normalize(hidden_rows)
        scaled_grad = dpooled * pool_scale
        grad_gain = lax.optimization_barrier(jnp.sum(scaled_grad * lax.optimization_barrier(jnp.sum(normed, axis=1)), axis=0))
        dnorm = (scaled_grad * gains)[:, None, :]
        grad_hidden = inverse_rms * (dnorm - normed * lax.optimization_barrier(jnp.mean(dnorm * normed, axis=-1, keepdims=True)))
        return (grad_hidden.astype(jnp.bfloat16), note_loss, grad_gain)
    model_ids = jnp.arange(MODELS, dtype=jnp.int32)
    grad_hidden, note_loss, grad_gain = lax.map(backward, (hidden, gain, head, partner, model_ids))
    return (grad_hidden, note_loss, grad_gain)
```

```python
import functools
import math

import jax
import jax.numpy as jnp
from jax import lax
from jax.experimental import pallas as pl
from jax.experimental.pallas import tpu as pltpu
from jax.sharding import PartitionSpec as P

MESH = pl.DeviceIdType.MESH
EPS = 1e-05
LC = 768
ROWS = 16
ORDER = ((0, 0), (1, 0), (1, 1), (0, 1))
SKEW = dict(edge=2, cross=4, back=6, ew=8, m2=10)


def kernel(
    K, steps_per, partner, gain, hidden, codes, head,
    out_hidden, out_loss, out_gain,
    hv, ht, pb, lg, db, dl, dp, rss, rsr, xs, es, ns, inv, la, ls, lr, lrr,
    cb, cr, clb, clr, acc, accl, tg, gg, rank, sel, *rest,
):
    S = 4 * steps_per
    za, zc = rest[:S], rest[S : 2 * S]
    (hsem, ag_s, ag_r, y_s, y_r, z_s, z_r, b_s, b_r, l_s, l_r, r_s, r_r, q_s, q_r, c_s, c_r, g_s, g_r) = rest[2 * S :]
    mp, f = lax.axis_index("mp"), lax.axis_index("fsdp")
    y, z = mp // 4, lax.rem(mp, 4)
    h, x, core = f // 8, lax.rem(f, 8) // 2, lax.rem(f, 2)
    half = z // 2
    edge = lax.rem(z + 1, 4) < 2
    inner = jnp.logical_not(edge)
    zin, zout = 1 + half, 3 * half
    sends = []

    def start(src, dst, ssem, rsem, dev, when=None):
        def go():
            pltpu.make_async_remote_copy(src, dst, ssem, rsem, device_id=dev, device_id_type=MESH).start()

        def end():
            pltpu.make_async_remote_copy(src, dst, ssem, rsem, device_id=dev, device_id_type=MESH).wait_send()

        if when is None:
            go()
            sends.append(end)
        else:
            pl.when(when)(go)
            sends.append(lambda: pl.when(when)(end))

    def arrived(dst, rsem, when=None):
        def go():
            pltpu.make_async_remote_copy(dst, dst, rsem, rsem, device_id={"mp": mp, "fsdp": lax.rem(f + 1, 16)}, device_id_type=MESH).wait_recv()

        if when is None:
            go()
        else:
            pl.when(when)(go)

    def ydev(d):
        return lax.rem(y + d, 4)

    loads = []
    for lc in range(steps_per):
        c = pltpu.make_async_copy(head.at[0, :, pl.ds(lc * LC, LC)], hv.at[lc], hsem.at[lc])
        c.start()
        loads.append(c)

    bar = pltpu.get_barrier_semaphore()
    for i in range(1, 16):
        pl.semaphore_signal(bar, inc=1, device_id={"fsdp": lax.rem(f + i, 16)}, device_id_type=MESH)
    for d in (1, 2, 3):
        pl.semaphore_signal(bar, inc=1, device_id={"mp": ydev(d) * 4 + z}, device_id_type=MESH)

    @pl.when(edge)
    def _():
        pl.semaphore_signal(bar, inc=1, device_id={"mp": y * 4 + zin}, device_id_type=MESH)

    @pl.when(inner)
    def _():
        pl.semaphore_signal(bar, inc=1, device_id={"mp": y * 4 + zout}, device_id_type=MESH)
        pl.semaphore_signal(bar, inc=1, device_id={"mp": y * 4 + 3 - z}, device_id_type=MESH)

    def pool(n, _):
        states = hidden[0, n].astype(jnp.float32)
        r = lax.rsqrt(jnp.mean(states * states, axis=-1, keepdims=True) + EPS)
        inv[n] = jnp.broadcast_to(r, (16, 128))
        ns[pl.ds(n, 1), :] = jnp.sum(states * r, axis=0, keepdims=True)
        return 0

    lax.fori_loop(0, ROWS, pool, 0)
    pb[core, x] = (ns[...] * gain[...] * 0.25).astype(jnp.bfloat16)

    for hh in range(2):
        r = jnp.int32(0)
        for o in range(8):
            m = 4 * (o % 4) + (1 + hh if o < 4 else 3 * hh)
            rank[m] = r
            r = r + (((partner[m] & 3) >> 1) ^ hh)

    def place(p):
        pz, py = p & 3, p >> 2
        return jnp.where(pz == zin, py, jnp.where(pz == zout, 4 + py, 8 + rank[p]))

    for j in range(4):
        p = partner[4 * j + z]
        sel[j] = jnp.where(edge, jnp.where((p & 3) == z, p >> 2, 4 + j), place(p))
        p = partner[4 * j + zout]
        sel[4 + j] = jnp.where((p & 3) == zout, 0, place(p))
    picks = [jnp.int32(0)] * K
    for o in range(8):
        m = 4 * (o % 4) + (zin if o < 4 else zout)
        away = ((partner[m] & 3) >> 1) != half
        for j in range(K):
            picks[j] = jnp.where(jnp.logical_and(away, rank[m] == j), o, picks[j])
    for j in range(K):
        sel[8 + j] = picks[j]

    @pl.when(edge)
    def _():
        pl.semaphore_wait(bar, 19)

    @pl.when(inner)
    def _():
        pl.semaphore_wait(bar, 20)

    def mates(c, lo, when):
        i = lo
        for dx, dc in ((0, 1), (1, 0), (3, 0), (1, 1), (3, 1), (2, 0), (2, 1)):
            dev = {"fsdp": h * 8 + lax.rem(x + dx, 4) * 2 + lax.rem(core + dc, 2)}
            start(pb.at[c, x], pb.at[c, x], ag_s.at[i], ag_r.at[c, x], dev, when)
            i += 1

    other = {"fsdp": lax.rem(f + 8, 16)}
    start(pb.at[core, x], pb.at[2 + core, x], ag_s.at[0], ag_r.at[2 + core, x], other)
    mates(core, 1, core == 0)

    for lc in range(steps_per):
        loads[lc].wait()

        def turn(i, _):
            r = pl.multiple_of(i * 256, 256)
            ht[lc, :, pl.ds(r, 256)] = hv[lc, pl.ds(r, 256), :].T
            return 0

        lax.fori_loop(0, 8, turn, 0)

    def stage_m1(s):
        ci, lc = s // steps_per, s % steps_per
        rel, cc = ORDER[ci]
        c = rel * 2 + cc
        if lc == 0:
            for i in range(4):
                mine = jnp.logical_and(core == cc, x == i)
                arrived(pb.at[c, i], ag_r.at[c, i], jnp.logical_not(mine))
        v = jnp.dot(pb[c].reshape(64, pb.shape[3]), hv[lc], preferred_element_type=jnp.float32).astype(jnp.bfloat16)
        for i in range(4):
            lg[s, i] = v[i * 16 : (i + 1) * 16]
        za[s][y] = lg[s, y]
        for d in (1, 3, 2):
            start(lg.at[s, ydev(d)], za[s].at[y], y_s.at[s, d], y_r.at[s, y], {"mp": ydev(d) * 4 + z})

    def stage_edge(s):
        for d in (1, 3, 2):
            arrived(za[s].at[ydev(d)], y_r.at[s, ydev(d)])
        start(za[s].at[pl.ds(0, 4)], za[s].at[pl.ds(4, 4)], z_s.at[s, 0], z_r.at[s, 0], {"mp": y * 4 + zin}, edge)

    def fetch(s, i):
        a = za[s][jnp.minimum(i, 7)]
        b = zc[s][jnp.maximum(i - 8, 0)]
        return jnp.where(i < 8, a, b)

    def stage_cross(s):
        @pl.when(inner)
        def _():
            arrived(za[s].at[pl.ds(4, 4)], z_r.at[s, 0])
            for j in range(K):
                xs[s, j] = za[s][sel[8 + j]]

        start(xs.at[s], zc[s], z_s.at[s, 1], z_r.at[s, 1], {"mp": y * 4 + 3 - z}, inner)

    def stage_back(s):
        @pl.when(inner)
        def _():
            arrived(zc[s], z_r.at[s, 1])
            for j in range(4):
                es[s, j] = fetch(s, sel[4 + j])

        start(es.at[s], za[s].at[pl.ds(4, 4)], z_s.at[s, 0], z_r.at[s, 0], {"mp": y * 4 + zout}, inner)

    def stage_ew(s):
        ci, lc = s // steps_per, s % steps_per
        rel, cc = ORDER[ci]
        arrived(za[s].at[pl.ds(4, 4)], z_r.at[s, 0], edge)
        hc = h if rel == 0 else 1 - h
        row = pl.multiple_of((hc * 8 + y * 2 + cc) * 16, 16)
        ids = codes[pl.ds(row, 16), :] - (f * (LC * steps_per) + lc * LC)
        lanes = lax.broadcasted_iota(jnp.int32, (16, LC), 1)
        hit = ids[:, 0:1] == lanes
        for j in range(1, 16):
            hit = jnp.logical_or(hit, ids[:, j : j + 1] == lanes)
        tg[...] = jnp.where(hit, 1.0, 0.0)

        def model(j, _):
            i = sel[j]
            a = za[s][jnp.minimum(i, 7)]
            b = zc[s][jnp.maximum(i - 8, 0)]
            q = jnp.where(i < 8, a, b).astype(jnp.float32)
            v = za[s][j].astype(jnp.float32)
            target = tg[...]
            e = jnp.exp(jnp.abs(v) * -0.5)
            e2 = e * e
            a1, b1 = 1.0 + e, 1.0 + e2
            rr = 1.0 / (a1 * b1)
            pos = v >= 0.0
            s12 = (jnp.where(pos, 1.0, e2) * a1 + jnp.where(pos, 1.0, e) * b1) * rr
            t = 1.0 / (1.0 + jnp.exp(q * -0.5))
            db[s, j] = (s12 - target - t).astype(jnp.bfloat16)
            each = 2.0 * jnp.maximum(v, 0.0) + jnp.log(a1 * a1 * b1) - (t + target) * v
            part = each[:, 0:128]
            for k in range(128, LC, 128):
                part = part + each[:, k : k + 128]
            if lc == 0:
                la[ci, j] = part
            else:
                la[ci, j] += part
            return 0

        lax.fori_loop(0, 4, model, 0)
        dl[s, y] = db[s, y]
        for d in (1, 3, 2):
            start(db.at[s, ydev(d)], dl.at[s, y], b_s.at[s, d], b_r.at[s, y], {"mp": ydev(d) * 4 + z})
        if lc == steps_per - 1:
            diag = lax.broadcasted_iota(jnp.int32, (16, 128), 0) == lax.broadcasted_iota(jnp.int32, (16, 128), 1)
            for j in range(4):
                total = jnp.sum(la[ci, j], axis=1, keepdims=True)
                line = jnp.sum(jnp.where(diag, total, 0.0), axis=0, keepdims=True)
                ls[ci, j] = jnp.broadcast_to(line, (8, 128))
            lr[ci, y] = ls[ci, y]
            for d in (1, 3, 2):
                start(ls.at[ci, ydev(d)], lr.at[ci, y], l_s.at[ci, d], l_r.at[ci, y], {"mp": ydev(d) * 4 + z})

    def stage_m2(s):
        ci, lc = s // steps_per, s % steps_per
        rel, cc = ORDER[ci]
        c = rel * 2 + cc
        for d in (1, 3, 2):
            arrived(dl.at[s, ydev(d)], b_r.at[s, ydev(d)])
        left = dl[s].reshape(64, LC)
        for n in range(0, 2048, 1024):
            v = jnp.dot(left, ht[lc, :, n : n + 1024], preferred_element_type=jnp.float32)
            for i in range(4):
                w = v[i * 16 : (i + 1) * 16]
                if lc > 0:
                    w = w + dp[c, i, :, n : n + 1024]
                dp[c, i, :, n : n + 1024] = w
                if lc == steps_per - 1:
                    rss[ci, i, :, n : n + 1024] = w.astype(jnp.bfloat16)
        if lc == steps_per - 1:
            me = x * 2 + core
            for dx in (1, 3, 2, 0):
                xx = lax.rem(x + dx, 4)
                dev = {"fsdp": h * 8 + xx * 2 + cc}
                when = None if dx else core != cc
                start(rss.at[ci, xx], rsr.at[rel, me], r_s.at[ci, dx], r_r.at[rel, me], dev, when)
            for d in (1, 3, 2):
                arrived(lr.at[ci, ydev(d)], l_r.at[ci, ydev(d)])
            for dx in (1, 3, 2, 0):
                xx = lax.rem(x + dx, 4)
                dev = {"fsdp": h * 8 + xx * 2 + cc}
                when = None if dx else core != cc
                start(lr.at[ci, xx], lrr.at[rel, me], q_s.at[ci, dx], q_r.at[rel, me], dev, when)

    def gather_sum(rel):
        ci = jnp.where(core == 0, ORDER.index((rel, 0)), ORDER.index((rel, 1)))
        me = x * 2 + core
        acc[...] = dp[rel * 2 + core, x]
        accl[...] = lr[ci, x]
        for i in range(1, 8):
            src = lax.rem(me + i, 8)
            arrived(rsr.at[rel, src], r_r.at[rel, src])
            acc[...] += rsr[rel, src].astype(jnp.float32)
        for i in range(1, 8):
            src = lax.rem(me + i, 8)
            arrived(lrr.at[rel, src], q_r.at[rel, src])
            accl[...] += lrr[rel, src]

    for t in range(S + SKEW["m2"]):
        if t < S:
            stage_m1(t)
        if t == steps_per - 1:
            arrived(pb.at[2 + core, x], ag_r.at[2 + core, x])
            mates(2 + core, 8, None)
            mates(core, 1 + 14, core == 1)
        for name, fn in (("edge", stage_edge), ("cross", stage_cross), ("back", stage_back), ("ew", stage_ew), ("m2", stage_m2)):
            s = t - SKEW[name]
            if 0 <= s < S:
                fn(s)
                if name == "m2" and s == S - 2:
                    gather_sum(1)
                    cb[...] = acc[...].astype(jnp.bfloat16)
                    clb[...] = accl[...]
                    start(cb, cr, c_s.at[0], c_r.at[0], other)
                    start(clb, clr, c_s.at[1], c_r.at[1], other)

    gather_sum(0)
    arrived(cr, c_r.at[0])
    arrived(clr, c_r.at[1])
    acc[...] = (acc[...] + cr[...].astype(jnp.float32)) * 0.25
    out_loss[...] = (accl[...] + clr[...]) * (1.0 / (LC * steps_per * 16))
    gg[f] = jnp.sum(acc[...] * ns[...], axis=0, keepdims=True)
    for i in range(1, 16):
        start(gg.at[f], gg.at[f], g_s.at[i], g_r.at[f], {"fsdp": lax.rem(f + i, 16)})

    def final(n, _):
        dn = acc[pl.ds(n, 1), :] * gain[...]
        r = inv[n][:, 0:1]
        nm = hidden[0, n].astype(jnp.float32) * r
        mean = jnp.mean(dn * nm, axis=-1, keepdims=True)
        out_hidden[0, n] = (r * (dn - nm * mean)).astype(jnp.bfloat16)
        return 0

    lax.fori_loop(0, ROWS, final, 0)
    for i in range(1, 16):
        src = lax.rem(f + i, 16)
        arrived(gg.at[src], g_r.at[src])
    total = gg[0]
    for i in range(1, 16):
        total = total + gg[i]
    out_gain[...] = total
    for end in sends:
        end()


def call(K, cid, hidden, gain, head, partner, codes):
    D = hidden.shape[3]
    steps_per = head.shape[2] // LC
    S = 4 * steps_per
    bf, f32 = jnp.bfloat16, jnp.float32
    V, dma = pltpu.VMEM, pltpu.SemaphoreType.DMA
    vmem = pl.BlockSpec(memory_space=pltpu.VMEM)
    scratch = [
        V((steps_per, D, LC), bf), V((steps_per, LC, D), bf), V((4, 4, 16, D), bf),
        V((S, 4, 16, LC), bf), V((S, 4, 16, LC), bf), V((S, 4, 16, LC), bf),
        V((4, 4, 16, D), f32), V((4, 4, 16, D), bf), V((2, 8, 16, D), bf),
        V((S, K, 16, LC), bf), V((S, 4, 16, LC), bf),
        V((16, D), f32), V((16, 16, 128), f32), V((4, 4, 16, 128), f32),
        V((4, 4, 8, 128), f32), V((4, 4, 8, 128), f32), V((2, 8, 8, 128), f32),
        V((16, D), bf), V((16, D), bf), V((8, 128), f32), V((8, 128), f32),
        V((16, D), f32), V((8, 128), f32), V((16, LC), f32), V((16, 1, D), f32),
        pltpu.SMEM((16,), jnp.int32), pltpu.SMEM((8 + K,), jnp.int32),
    ]
    scratch += [V((8, 16, LC), bf) for _ in range(S)]
    scratch += [V((K, 16, LC), bf) for _ in range(S)]
    scratch += [
        dma((steps_per,)), dma((22,)), dma((4, 4)), dma((S, 4)), dma((S, 4)), dma((S, 2)), dma((S, 2)),
        dma((S, 4)), dma((S, 4)), dma((4, 4)), dma((4, 4)), dma((4, 4)), dma((2, 8)), dma((4, 4)), dma((2, 8)),
        dma((2,)), dma((2,)), dma((16,)), dma((16,)),
    ]
    return pl.pallas_call(
        functools.partial(kernel, K, steps_per),
        name="distill%d" % K,
        out_shape=(
            jax.ShapeDtypeStruct(hidden.shape, bf),
            jax.ShapeDtypeStruct((8, 128), f32),
            jax.ShapeDtypeStruct((1, D), f32),
        ),
        in_specs=[pl.BlockSpec(memory_space=pltpu.SMEM), vmem, vmem, vmem, pl.BlockSpec(memory_space=pl.ANY)],
        out_specs=(vmem, vmem, vmem),
        scratch_shapes=scratch,
        compiler_params=pltpu.CompilerParams(
            collective_id=cid, has_side_effects=True, vmem_limit_bytes=60 * 2**20
        ),
    )(partner, gain, hidden, codes, head)


def on_device(hidden, gain, head, partner, codes):
    grad_hidden, loss, grad_gain = call(8, 1, hidden, gain, head, partner, codes)
    return grad_hidden, loss[0:1, 0:16], grad_gain


def solution(mesh):
    return jax.shard_map(
        on_device,
        mesh=mesh,
        in_specs=(P("mp", "fsdp", None, None), P("mp", None), P("mp", None, "fsdp"), P(), P()),
        out_specs=(P("mp", "fsdp", None, None), P("mp", "fsdp"), P("mp", None)),
        check_vma=False,
    )
```

```python
import functools
import math

import jax
import jax.numpy as jnp
from jax import lax
from jax.experimental import pallas as pl
from jax.experimental.pallas import tpu as pltpu
from jax.sharding import PartitionSpec as P

MESH = pl.DeviceIdType.MESH
EPS = 1e-05
LC = 768
ROWS = 16
SIZES = (4, 8)
EDGE, CROSS, BACK, EW, M2 = 2, 4, 6, 8, 10


def kernel(
    K, per, partner, gain, codes, hidden, head,
    out_acc, out_loss, out_gain, inv,
    hs, ct, hv, ht, pb, lg, db, dl, dp, rss, rsr, xs, es, ns, la, ls, lr, lrr,
    cb, cr, clb, clr, accl, tg, gg, za, zc, rank, sel,
    isem, hsem, ag_s, ag_r, y_s, y_r, z_s, z_r, b_s, b_r, l_s, l_r, r_s, r_r, q_s, q_r, c_s, c_r, g_s, g_r,
):
    S = 4 * per
    mp, f = lax.axis_index("mp"), lax.axis_index("fsdp")
    y, z = mp // 4, lax.rem(mp, 4)
    h, x, core = f // 8, lax.rem(f, 8) // 2, lax.rem(f, 2)
    half = z // 2
    edge = lax.rem(z + 1, 4) < 2
    inner = jnp.logical_not(edge)
    zin, zout = 1 + half, 3 * half
    me = x * 2 + core
    other = {"fsdp": lax.rem(f + 8, 16)}
    sibling = {"fsdp": f + 1 - 2 * core}

    def remote(src, dst, ssem, rsem, dev):
        return pltpu.make_async_remote_copy(src, dst, ssem, rsem, device_id=dev, device_id_type=MESH)

    def start(*copy):
        remote(*copy).start()

    def arrived(dst, rsem):
        remote(dst, dst, rsem, rsem, other).wait_recv()

    def sent(src, ssem):
        remote(src, src, ssem, ssem, other).wait_send()

    def loop(n, body):
        def step(i, _):
            body(i)
            return 0

        lax.fori_loop(0, n, step, 0)

    def chunk(ci):
        return lax.rem((ci + 1) // 2, 2), ci // 2

    def ydev(d):
        return lax.rem(y + d, 4)

    def mate(d):
        return {"mp": ydev(d) * 4 + z}

    whole_hidden = pltpu.make_async_copy(hidden.at[0], hs, isem)
    whole_hidden.start()

    def head_part(lc):
        return pltpu.make_async_copy(head.at[0, :, pl.ds(pl.multiple_of(lc * LC, 128), LC)], hv.at[lc], hsem.at[lc])

    loop(per, lambda lc: head_part(lc).start())

    bar = pltpu.get_barrier_semaphore()

    def greet(dev):
        pl.semaphore_signal(bar, inc=1, device_id=dev, device_id_type=MESH)

    loop(15, lambda i: greet({"fsdp": lax.rem(f + i + 1, 16)}))
    loop(3, lambda i: greet(mate(i + 1)))

    @pl.when(edge)
    def _():
        greet({"mp": y * 4 + zin})

    @pl.when(inner)
    def _():
        greet({"mp": y * 4 + zout})
        greet({"mp": y * 4 + 3 - z})

    for hh in range(2):
        r = jnp.int32(0)
        for o in range(8):
            m = 4 * (o % 4) + (1 + hh if o < 4 else 3 * hh)
            rank[m] = r
            r = r + (((partner[m] & 3) >> 1) ^ hh)

    def place(p):
        pz, py = p & 3, p >> 2
        return jnp.where(pz == zin, py, jnp.where(pz == zout, 4 + py, 8 + rank[p]))

    def find(j):
        p = partner[4 * j + z]
        sel[j] = jnp.where(edge, jnp.where((p & 3) == z, p >> 2, 4 + j), place(p))
        p = partner[4 * j + zout]
        sel[4 + j] = jnp.where((p & 3) == zout, 0, place(p))

    loop(4, find)

    def pick(j):
        got = jnp.int32(0)
        for o in range(8):
            m = 4 * (o % 4) + (zin if o < 4 else zout)
            away = ((partner[m] & 3) >> 1) != half
            got = jnp.where(jnp.logical_and(away, rank[m] == j), o, got)
        sel[8 + j] = got

    loop(K, pick)

    whole_hidden.wait()

    def pool(n, _):
        states = hs[n].astype(jnp.float32)
        r = lax.rsqrt(jnp.mean(states * states, axis=-1, keepdims=True) + EPS)
        inv[n] = jnp.broadcast_to(r, (16, 128))
        ns[pl.ds(n, 1), :] = jnp.sum(states * r, axis=0, keepdims=True)
        return 0

    lax.fori_loop(0, ROWS, pool, 0, unroll=4)
    pb[core, x] = (ns[...] * gain[...] * 0.25).astype(jnp.bfloat16)

    @pl.when(edge)
    def _():
        pl.semaphore_wait(bar, 19)

    @pl.when(inner)
    def _():
        pl.semaphore_wait(bar, 20)

    def spread(c, i):
        for k, dx in enumerate((1, 3, 2)):
            start(pb.at[c, x], pb.at[c, x], ag_s.at[i + k], ag_r.at[c, x], {"fsdp": h * 8 + lax.rem(x + dx, 4) * 2 + core})
        start(pb.at[c, x], pb.at[c, x], ag_s.at[i + 3], ag_r.at[c, x], sibling)

    def hand_on(c, i):
        for k, dx in enumerate((1, 3, 2)):
            xx = lax.rem(x + dx, 4)
            arrived(pb.at[c, xx], ag_r.at[c, xx])
            start(pb.at[c, xx], pb.at[c, xx], ag_s.at[i + k], ag_r.at[c, xx], sibling)

    start(pb.at[core, x], pb.at[2 + core, x], ag_s.at[0], ag_r.at[2 + core, x], other)
    spread(core, 1)

    ct[...] = codes[...].T
    la[...] = jnp.zeros_like(la)
    gg[f] = jnp.zeros_like(gg[f])

    def clear(i):
        dp[i // 4, lax.rem(i, 4)] = jnp.zeros(dp.shape[2:], jnp.float32)

    loop(16, clear)

    def turn(lc):
        head_part(lc).wait()

        def part(i):
            r = pl.multiple_of(i * 256, 256)
            ht[lc, :, pl.ds(r, 256)] = hv[lc, pl.ds(r, 256), :].T

        loop(8, part)

        @pl.when(lc == 0)
        def _():
            hand_on(core, 5)

    loop(per, turn)

    def stage_m1(s):
        ci = s // per
        lc = s - ci * per
        rel, cc = chunk(ci)
        c = rel * 2 + cc

        @pl.when(jnp.logical_and(lc == 0, core != cc))
        def _():
            loop(4, lambda i: arrived(pb.at[c, i], ag_r.at[c, i]))

        v = jnp.dot(pb[c].reshape(64, pb.shape[3]), hv[lc], preferred_element_type=jnp.float32).astype(jnp.bfloat16)
        for i in range(4):
            lg[s, i] = v[i * 16 : (i + 1) * 16]
        za[s, y] = lg[s, y]
        for d in (1, 3, 2):
            start(lg.at[s, ydev(d)], za.at[s, y], y_s.at[s, d], y_r.at[s, y], mate(d))

    def outer(s):
        return za.at[s, pl.ds(4, 4)]

    def stage_edge(s):
        loop(3, lambda i: arrived(za.at[s, ydev(i + 1)], y_r.at[s, ydev(i + 1)]))

        @pl.when(edge)
        def _():
            start(za.at[s, pl.ds(0, 4)], outer(s), z_s.at[s, 0], z_r.at[s, 0], {"mp": y * 4 + zin})

    def fetch(s, i, n):
        got = za[s, 0]
        for k in range(1, n):
            got = jnp.where(i == k, za[s, k] if k < 8 else zc[s, k - 8], got)
        return got

    def stage_cross(s):
        @pl.when(inner)
        def _():
            arrived(outer(s), z_r.at[s, 0])

            def put(j):
                xs[s, j] = fetch(s, sel[8 + j], 8)

            loop(K, put)
            start(xs.at[s], zc.at[s], z_s.at[s, 1], z_r.at[s, 1], {"mp": y * 4 + 3 - z})

    def stage_back(s):
        @pl.when(inner)
        def _():
            arrived(zc.at[s], z_r.at[s, 1])

            def put(j):
                es[s, j] = fetch(s, sel[4 + j], 8 + K)

            loop(4, put)
            start(es.at[s], outer(s), z_s.at[s, 0], z_r.at[s, 0], {"mp": y * 4 + zout})

    def stage_ew(s):
        ci = s // per
        lc = s - ci * per
        rel, cc = chunk(ci)

        @pl.when(edge)
        def _():
            arrived(outer(s), z_r.at[s, 0])

        hc = jnp.where(rel == 0, h, 1 - h)
        row = pl.multiple_of((hc * 8 + y * 2 + cc) * 16, 16)
        ids = ct[pl.ds(row, 16), :] - (f * (LC * per) + lc * LC)
        lanes = lax.broadcasted_iota(jnp.int32, (16, LC), 1)
        hit = ids[:, 0:1] == lanes
        for j in range(1, 16):
            hit = jnp.logical_or(hit, ids[:, j : j + 1] == lanes)
        tg[...] = jnp.where(hit, 1.0, 0.0)

        def model(j):
            q = fetch(s, sel[j], 8 + K).astype(jnp.float32)
            v = za[s, j].astype(jnp.float32)
            target = tg[...]
            e = jnp.exp(jnp.abs(v) * -0.5)
            e2 = e * e
            a1, b1 = 1.0 + e, 1.0 + e2
            rr = 1.0 / (a1 * b1)
            pos = v >= 0.0
            s12 = (jnp.where(pos, 1.0, e2) * a1 + jnp.where(pos, 1.0, e) * b1) * rr
            t = 1.0 / (1.0 + jnp.exp(q * -0.5))
            db[s, j] = (s12 - target - t).astype(jnp.bfloat16)
            each = 2.0 * jnp.maximum(v, 0.0) + jnp.log(a1 * a1 * b1) - (t + target) * v
            part = each[:, 0:128]
            for k in range(128, LC, 128):
                part = part + each[:, k : k + 128]
            la[ci, j] += part

        loop(4, model)
        dl[s, y] = db[s, y]
        for d in (1, 3, 2):
            start(db.at[s, ydev(d)], dl.at[s, y], b_s.at[s, d], b_r.at[s, y], mate(d))

        @pl.when(lc == per - 1)
        def _():
            diag = lax.broadcasted_iota(jnp.int32, (16, 128), 0) == lax.broadcasted_iota(jnp.int32, (16, 128), 1)

            def line(j):
                total = jnp.sum(la[ci, j], axis=1, keepdims=True)
                row = jnp.sum(jnp.where(diag, total, 0.0), axis=0, keepdims=True)
                ls[ci, j] = jnp.broadcast_to(row, (8, 128))

            loop(4, line)
            lr[ci, y] = ls[ci, y]
            for d in (1, 3, 2):
                start(ls.at[ci, ydev(d)], lr.at[ci, y], l_s.at[ci, d], l_r.at[ci, y], mate(d))

    def owner(dx, cc):
        xx = lax.rem(x + dx, 4)
        return xx, {"fsdp": h * 8 + xx * 2 + cc}

    def stage_m2(s):
        ci = s // per
        lc = s - ci * per
        rel, cc = chunk(ci)
        c = rel * 2 + cc
        loop(3, lambda i: arrived(dl.at[s, ydev(i + 1)], b_r.at[s, ydev(i + 1)]))
        left = dl[s].reshape(64, LC)
        for n in range(0, 2048, 1024):
            v = jnp.dot(left, ht[lc, :, n : n + 1024], preferred_element_type=jnp.float32)
            for i in range(4):
                dp[c, i, :, n : n + 1024] += v[i * 16 : (i + 1) * 16]

        @pl.when(lc == per - 1)
        def _():
            def turn_in(i):
                w = dp[c, i]
                rss[ci, i] = w.astype(jnp.bfloat16)
                gg[f] += jnp.sum(w * pb[c, i].astype(jnp.float32), axis=0, keepdims=True)

            loop(4, turn_in)

            def give(dx):
                xx, dev = owner(dx, cc)
                start(rss.at[ci, xx], rsr.at[rel, me], r_s.at[ci, dx], r_r.at[rel, me], dev)

            def give_loss(dx):
                xx, dev = owner(dx, cc)
                start(lr.at[ci, xx], lrr.at[rel, me], q_s.at[ci, dx], q_r.at[rel, me], dev)

            loop(3, lambda i: give(i + 1))
            pl.when(core != cc)(lambda: give(0))
            loop(3, lambda i: arrived(lr.at[ci, ydev(i + 1)], l_r.at[ci, ydev(i + 1)]))
            loop(3, lambda i: give_loss(i + 1))
            pl.when(core != cc)(lambda: give_loss(0))

    def gather_sum(rel):
        ci = jnp.where(core == 0, rel, 3 - rel)
        out_acc[...] = dp[rel * 2 + core, x]
        accl[...] = lr[ci, x]

        def add(i):
            src = lax.rem(me + 1 + i, 8)
            arrived(rsr.at[rel, src], r_r.at[rel, src])
            out_acc[...] += rsr[rel, src].astype(jnp.float32)
            arrived(lrr.at[rel, src], q_r.at[rel, src])
            accl[...] += lrr[rel, src]

        loop(7, add)

    def stage(t, lag, fn):
        pl.when(jnp.logical_and(t >= lag, t < S + lag))(lambda: fn(t - lag))

    def tick(t):
        pl.when(t < S)(lambda: stage_m1(t))

        @pl.when(t == 0)
        def _():
            arrived(pb.at[2 + core, x], ag_r.at[2 + core, x])
            spread(2 + core, 8)

        @pl.when(t == per - 1)
        def _():
            hand_on(2 + core, 12)

        stage(t, EDGE, stage_edge)
        stage(t, CROSS, stage_cross)
        stage(t, BACK, stage_back)
        stage(t, EW, stage_ew)
        stage(t, M2, stage_m2)

        @pl.when(t == S - 2 + M2)
        def _():
            gather_sum(1)
            cb[...] = out_acc[...].astype(jnp.bfloat16)
            clb[...] = accl[...]
            start(cb, cr, c_s.at[0], c_r.at[0], other)
            start(clb, clr, c_s.at[1], c_r.at[1], other)

    loop(S + M2, tick)

    loop(15, lambda i: start(gg.at[f], gg.at[f], g_s.at[i + 1], g_r.at[f], {"fsdp": lax.rem(f + 1 + i, 16)}))
    gather_sum(0)
    arrived(cr, c_r.at[0])
    arrived(clr, c_r.at[1])
    out_acc[...] = (out_acc[...] + cr[...].astype(jnp.float32)) * 0.25
    out_loss[...] = (accl[...] + clr[...]) * (1.0 / (LC * per * 16))
    out_gain[...] = gg[f]

    def add_gain(i):
        src = lax.rem(f + 1 + i, 16)
        arrived(gg.at[src], g_r.at[src])
        out_gain[...] += gg[src]

    loop(15, add_gain)
    out_gain[...] = out_gain[...] / gain[...]

    loop(15, lambda i: sent(pb.at[0, 0], ag_s.at[i]))
    loop(15, lambda i: sent(gg.at[f], g_s.at[i + 1]))
    sent(cb, c_s.at[0])
    sent(clb, c_s.at[1])

    def step_left(s):
        for d in (1, 2, 3):
            sent(lg.at[s, 0], y_s.at[s, d])
            sent(db.at[s, 0], b_s.at[s, d])
        sent(es.at[s], z_s.at[s, 0])
        pl.when(inner)(lambda: sent(xs.at[s], z_s.at[s, 1]))

    loop(S, step_left)

    def chunk_left(ci):
        def both(dx):
            sent(rss.at[ci, 0], r_s.at[ci, dx])
            sent(lr.at[ci, 0], q_s.at[ci, dx])

        for d in (1, 2, 3):
            sent(ls.at[ci, 0], l_s.at[ci, d])
            both(d)
        pl.when(core != ci // 2)(lambda: both(0))

    loop(4, chunk_left)


def call(K, cid, hidden, gain, head, partner, codes):
    D = hidden.shape[3]
    per = head.shape[2] // LC
    S = 4 * per
    bf, f32 = jnp.bfloat16, jnp.float32
    V, dma = pltpu.VMEM, pltpu.SemaphoreType.DMA
    vmem = pl.BlockSpec(memory_space=pltpu.VMEM)
    scratch = [
        V((16, 16, D), bf), V((256, 16), jnp.int32),
        V((per, D, LC), bf), V((per, LC, D), bf), V((4, 4, 16, D), bf),
        V((S, 4, 16, LC), bf), V((S, 4, 16, LC), bf), V((S, 4, 16, LC), bf),
        V((4, 4, 16, D), f32), V((4, 4, 16, D), bf), V((2, 8, 16, D), bf),
        V((S, K, 16, LC), bf), V((S, 4, 16, LC), bf),
        V((16, D), f32), V((4, 4, 16, 128), f32),
        V((4, 4, 8, 128), f32), V((4, 4, 8, 128), f32), V((2, 8, 8, 128), f32),
        V((16, D), bf), V((16, D), bf), V((8, 128), f32), V((8, 128), f32),
        V((8, 128), f32), V((16, LC), f32), V((16, 1, D), f32),
        V((S, 8, 16, LC), bf), V((S, K, 16, LC), bf),
        pltpu.SMEM((16,), jnp.int32), pltpu.SMEM((8 + K,), jnp.int32),
    ]
    scratch += [
        dma, dma((per,)), dma((15,)), dma((4, 4)), dma((S, 4)), dma((S, 4)), dma((S, 2)), dma((S, 2)),
        dma((S, 4)), dma((S, 4)), dma((4, 4)), dma((4, 4)), dma((4, 4)), dma((2, 8)), dma((4, 4)), dma((2, 8)),
        dma((2,)), dma((2,)), dma((16,)), dma((16,)),
    ]
    hbm = pl.BlockSpec(memory_space=pl.ANY)
    return pl.pallas_call(
        functools.partial(kernel, K, per),
        name="distill%d" % K,
        out_shape=(
            jax.ShapeDtypeStruct((16, D), f32),
            jax.ShapeDtypeStruct((8, 128), f32),
            jax.ShapeDtypeStruct((1, D), f32),
            jax.ShapeDtypeStruct((16, 16, 128), f32),
        ),
        in_specs=[pl.BlockSpec(memory_space=pltpu.SMEM), vmem, vmem, hbm, hbm],
        out_specs=(vmem, vmem, vmem, vmem),
        scratch_shapes=scratch,
        compiler_params=pltpu.CompilerParams(
            collective_id=cid, has_side_effects=True, vmem_limit_bytes=60 * 2**20
        ),
    )(partner, gain, codes, hidden, head)


def finish(acc, gain, inv, loss, total, hidden, out_hidden, out_loss, out_gain):
    g = gain[...]

    def note(n):
        dn = acc[n : n + 1, :] * g
        r = inv[n][:, 0:1]
        nm = hidden[0, n].astype(jnp.float32) * r
        mean = jnp.mean(dn * nm, axis=-1, keepdims=True)
        out_hidden[0, n] = (r * (dn - nm * mean)).astype(jnp.bfloat16)

    for n in range(8):
        note(n)

    @pl.when(pl.program_id(0) == 0)
    def _():
        out_loss[...] = loss[0:1, 0:16]
        out_gain[...] = total[...]


def last(acc, gain, inv, loss, total, hidden):
    D = hidden.shape[3]

    def whole(*shape):
        return pl.BlockSpec(shape, lambda i: (0,) * len(shape))

    block = pl.BlockSpec((1, 8, 16, D), lambda i: (0, i, 0, 0))
    return pl.pallas_call(
        finish,
        name="finish",
        grid=(2,),
        out_shape=(
            jax.ShapeDtypeStruct(hidden.shape, jnp.bfloat16),
            jax.ShapeDtypeStruct((1, 16), jnp.float32),
            jax.ShapeDtypeStruct((1, D), jnp.float32),
        ),
        in_specs=[
            pl.BlockSpec((8, D), lambda i: (i, 0)), whole(1, D), pl.BlockSpec((8, 16, 128), lambda i: (i, 0, 0)),
            whole(8, 128), whole(1, D), block,
        ],
        out_specs=(block, whole(1, 16), whole(1, D)),
    )(acc, gain, inv, loss, total, hidden)


def on_device(hidden, gain, head, partner, codes):
    ids = jnp.arange(16, dtype=jnp.int32)
    away = ((ids & 3) < 2) & ((partner & 3) >= 2)
    crossing = jnp.sum(away.astype(jnp.int32))
    args = (hidden, gain, head, partner, codes.T)
    calls = [functools.partial(call, K, i + 1) for i, K in enumerate(SIZES)]
    which = sum((crossing > K).astype(jnp.int32) for K in SIZES[:-1])
    acc, loss, total, inv = lax.switch(which, calls, *args) if len(SIZES) > 1 else calls[0](*args)
    return last(acc, gain, inv, loss, total, hidden)


def solution(mesh):
    return jax.shard_map(
        on_device,
        mesh=mesh,
        in_specs=(P("mp", "fsdp", None, None), P("mp", None), P("mp", None, "fsdp"), P(), P()),
        out_specs=(P("mp", "fsdp", None, None), P("mp", "fsdp"), P("mp", None)),
        check_vma=False,
    )
```

```python
import functools
import math

import jax
import jax.numpy as jnp
from jax import lax
from jax.experimental import pallas as pl
from jax.experimental.pallas import tpu as pltpu
from jax.sharding import PartitionSpec as P

MESH = pl.DeviceIdType.MESH
EPS = 1e-05
LC = 768
ROWS = 16
SIZES = (4, 6, 8)
EDGE, CROSS, BACK, EW, M2 = 2, 4, 6, 9, 11


def kernel(
    K, per, partner, gain, codes, hidden, head,
    out_acc, out_loss, out_gain, inv,
    hs, ct, hv, ht, pb, lg, db, dl, dp, rss, rsr, xs, es, ns, la, ls, lr, lrr,
    cb, cr, clb, clr, accl, tg, gg, za, zc, rank, sel,
    step_on, isem, hsem, ag_s, ag_r, y_s, y_r, z_s, z_r, b_s, b_r, l_s, l_r, r_s, r_r, q_s, q_r, c_s, c_r, g_s, g_r,
):
    S = 4 * per
    mp, f = lax.axis_index("mp"), lax.axis_index("fsdp")
    y, z = mp // 4, lax.rem(mp, 4)
    h, x, core = f // 8, lax.rem(f, 8) // 2, lax.rem(f, 2)
    half = z // 2
    edge = lax.rem(z + 1, 4) < 2
    inner = jnp.logical_not(edge)
    zin, zout = 1 + half, 3 * half
    me = x * 2 + core
    other = {"fsdp": lax.rem(f + 8, 16)}
    sibling = {"fsdp": f + 1 - 2 * core}

    def remote(src, dst, ssem, rsem, dev):
        return pltpu.make_async_remote_copy(src, dst, ssem, rsem, device_id=dev, device_id_type=MESH)

    def start(*copy):
        remote(*copy).start()

    def arrived(dst, rsem):
        remote(dst, dst, rsem, rsem, other).wait_recv()

    def sent(src, ssem):
        remote(src, src, ssem, ssem, other).wait_send()

    def loop(n, body):
        def step(i, _):
            body(i)
            return 0

        lax.fori_loop(0, n, step, 0)

    def chunk(ci):
        return lax.rem((ci + 1) // 2, 2), lax.rem(core + ci // 2, 2)

    def ydev(d):
        return lax.rem(y + d, 4)

    def mate(d):
        return {"mp": ydev(d) * 4 + z}

    whole_hidden = pltpu.make_async_copy(hidden.at[0], hs, isem)
    whole_hidden.start()

    def head_part(lc):
        return pltpu.make_async_copy(head.at[0, :, pl.ds(pl.multiple_of(lc * LC, 128), LC)], hv.at[lc], hsem.at[lc])

    loop(per, lambda lc: head_part(lc).start())

    bar = pltpu.get_barrier_semaphore()

    def greet(dev):
        pl.semaphore_signal(bar, inc=1, device_id=dev, device_id_type=MESH)

    loop(3, lambda i: greet({"fsdp": h * 8 + lax.rem(x + i + 1, 4) * 2 + core}))
    greet(sibling)
    loop(3, lambda i: greet(mate(i + 1)))
    up = {"mp": y * 4 + lax.rem(z + 1, 4), "fsdp": jnp.where(z == 3, lax.rem(f + 8, 16), f)}
    greet(up)
    greet({"mp": y * 4 + lax.rem(z + 3, 4), "fsdp": jnp.where(z == 0, lax.rem(f + 8, 16), f)})

    for hh in range(2):
        r = jnp.int32(0)
        for o in range(8):
            m = 4 * (o % 4) + (1 + hh if o < 4 else 3 * hh)
            rank[m] = r
            r = r + (((partner[m] & 3) >> 1) ^ hh)

    def place(p):
        pz, py = p & 3, p >> 2
        return jnp.where(pz == zin, py, jnp.where(pz == zout, 4 + py, 8 + rank[p]))

    def find(j):
        p = partner[4 * j + z]
        sel[j] = jnp.where(edge, jnp.where((p & 3) == z, p >> 2, 4 + j), place(p))
        p = partner[4 * j + zout]
        sel[4 + j] = jnp.where((p & 3) == zout, 0, place(p))

    loop(4, find)

    def pick(j):
        got = jnp.int32(0)
        for o in range(8):
            m = 4 * (o % 4) + (zin if o < 4 else zout)
            away = ((partner[m] & 3) >> 1) != half
            got = jnp.where(jnp.logical_and(away, rank[m] == j), o, got)
        sel[8 + j] = got

    loop(K, pick)

    whole_hidden.wait()

    def pool(n, _):
        states = hs[n].astype(jnp.float32)
        r = lax.rsqrt(jnp.mean(states * states, axis=-1, keepdims=True) + EPS)
        inv[n] = jnp.broadcast_to(r, (16, 128))
        ns[pl.ds(n, 1), :] = jnp.sum(states * r, axis=0, keepdims=True)
        return 0

    lax.fori_loop(0, ROWS, pool, 0, unroll=4)
    pb[core, x] = (ns[...] * gain[...] * 0.25).astype(jnp.bfloat16)

    pl.semaphore_wait(bar, 9)

    def spread(c, i):
        for k, dx in enumerate((1, 3, 2)):
            start(pb.at[c, x], pb.at[c, x], ag_s.at[i + k], ag_r.at[c, x], {"fsdp": h * 8 + lax.rem(x + dx, 4) * 2 + core})
        start(pb.at[c, x], pb.at[c, x], ag_s.at[i + 3], ag_r.at[c, x], sibling)

    def hand_on(c, i):
        for k, dx in enumerate((1, 3, 2)):
            xx = lax.rem(x + dx, 4)
            arrived(pb.at[c, xx], ag_r.at[c, xx])
            start(pb.at[c, xx], pb.at[c, xx], ag_s.at[i + k], ag_r.at[c, xx], sibling)

    def tell(i):
        pl.semaphore_signal(step_on.at[i], inc=1, device_id=up, device_id_type=MESH)

    tell(0)
    spread(core, 1)

    ct[...] = codes[...].T
    la[...] = jnp.zeros_like(la)
    gg[f] = jnp.zeros_like(gg[f])

    def clear(i):
        dp[i // 4, lax.rem(i, 4)] = jnp.zeros(dp.shape[2:], jnp.float32)

    loop(16, clear)

    def turn(lc):
        head_part(lc).wait()

        def part(i):
            r = pl.multiple_of(i * 256, 256)
            ht[lc, :, pl.ds(r, 256)] = hv[lc, pl.ds(r, 256), :].T

        loop(8, part)

    for i in range(3):
        if i < per:
            turn(i)
        pl.semaphore_wait(step_on.at[i], 1)
        if i < 2:
            tell(i + 1)
    start(pb.at[core, x], pb.at[2 + core, x], ag_s.at[0], ag_r.at[2 + core, x], other)
    for i in range(3, per):
        turn(i)
    hand_on(core, 5)

    def stage_m1(s):
        ci = s // per
        lc = s - ci * per
        rel, cc = chunk(ci)
        c = rel * 2 + cc

        @pl.when(jnp.logical_and(lc == 0, ci >= 2))
        def _():
            loop(4, lambda i: arrived(pb.at[c, i], ag_r.at[c, i]))

        v = jnp.dot(pb[c].reshape(64, pb.shape[3]), hv[lc], preferred_element_type=jnp.float32).astype(jnp.bfloat16)
        for i in range(4):
            lg[s, i] = v[i * 16 : (i + 1) * 16]
        za[s, y] = lg[s, y]
        for d in (1, 3, 2):
            start(lg.at[s, ydev(d)], za.at[s, y], y_s.at[s, d], y_r.at[s, y], mate(d))

    def outer(s):
        return za.at[s, pl.ds(4, 4)]

    def stage_edge(s):
        loop(3, lambda i: arrived(za.at[s, ydev(i + 1)], y_r.at[s, ydev(i + 1)]))

        @pl.when(edge)
        def _():
            start(za.at[s, pl.ds(0, 4)], outer(s), z_s.at[s, 0], z_r.at[s, 0], {"mp": y * 4 + zin})

    def fetch(s, i, n):
        got = za[s, 0]
        for k in range(1, n):
            got = jnp.where(i == k, za[s, k] if k < 8 else zc[s, k - 8], got)
        return got

    def stage_cross(s):
        @pl.when(inner)
        def _():
            arrived(outer(s), z_r.at[s, 0])

            def put(j):
                xs[s, j] = fetch(s, sel[8 + j], 8)

            loop(K, put)
            start(xs.at[s], zc.at[s], z_s.at[s, 1], z_r.at[s, 1], {"mp": y * 4 + 3 - z})

    def stage_back(s):
        @pl.when(inner)
        def _():
            arrived(zc.at[s], z_r.at[s, 1])

            def put(j):
                es[s, j] = fetch(s, sel[4 + j], 8 + K)

            loop(4, put)
            start(es.at[s], outer(s), z_s.at[s, 0], z_r.at[s, 0], {"mp": y * 4 + zout})

    def stage_ew(s):
        ci = s // per
        lc = s - ci * per
        rel, cc = chunk(ci)

        @pl.when(edge)
        def _():
            arrived(outer(s), z_r.at[s, 0])

        hc = jnp.where(rel == 0, h, 1 - h)
        row = pl.multiple_of((hc * 8 + y * 2 + cc) * 16, 16)
        ids = ct[pl.ds(row, 16), :] - (f * (LC * per) + lc * LC)
        lanes = lax.broadcasted_iota(jnp.int32, (16, LC), 1)
        hit = ids[:, 0:1] == lanes
        for j in range(1, 16):
            hit = jnp.logical_or(hit, ids[:, j : j + 1] == lanes)
        tg[...] = jnp.where(hit, 1.0, 0.0)

        def model(j):
            q = fetch(s, sel[j], 8 + K).astype(jnp.float32)
            v = za[s, j].astype(jnp.float32)
            target = tg[...]
            e = jnp.exp(jnp.abs(v) * -0.5)
            e2 = e * e
            a1, b1 = 1.0 + e, 1.0 + e2
            rr = 1.0 / (a1 * b1)
            pos = v >= 0.0
            s12 = (jnp.where(pos, 1.0, e2) * a1 + jnp.where(pos, 1.0, e) * b1) * rr
            t = 1.0 / (1.0 + jnp.exp(q * -0.5))
            db[s, j] = (s12 - target - t).astype(jnp.bfloat16)
            each = 2.0 * jnp.maximum(v, 0.0) + jnp.log(a1 * a1 * b1) - (t + target) * v
            part = each[:, 0:128]
            for k in range(128, LC, 128):
                part = part + each[:, k : k + 128]
            la[ci, j] += part

        loop(4, model)
        dl[s, y] = db[s, y]
        for d in (1, 3, 2):
            start(db.at[s, ydev(d)], dl.at[s, y], b_s.at[s, d], b_r.at[s, y], mate(d))

        @pl.when(lc == per - 1)
        def _():
            diag = lax.broadcasted_iota(jnp.int32, (16, 128), 0) == lax.broadcasted_iota(jnp.int32, (16, 128), 1)

            def line(j):
                total = jnp.sum(la[ci, j], axis=1, keepdims=True)
                row = jnp.sum(jnp.where(diag, total, 0.0), axis=0, keepdims=True)
                ls[ci, j] = jnp.broadcast_to(row, (8, 128))

            loop(4, line)
            lr[ci, y] = ls[ci, y]
            for d in (1, 3, 2):
                start(ls.at[ci, ydev(d)], lr.at[ci, y], l_s.at[ci, d], l_r.at[ci, y], mate(d))

    def owner(dx, cc):
        xx = lax.rem(x + dx, 4)
        return xx, {"fsdp": h * 8 + xx * 2 + cc}

    def stage_m2(s):
        ci = s // per
        lc = s - ci * per
        rel, cc = chunk(ci)
        c = rel * 2 + cc
        loop(3, lambda i: arrived(dl.at[s, ydev(i + 1)], b_r.at[s, ydev(i + 1)]))
        left = dl[s].reshape(64, LC)
        for n in range(0, 2048, 1024):
            v = jnp.dot(left, ht[lc, :, n : n + 1024], preferred_element_type=jnp.float32)
            for i in range(4):
                dp[c, i, :, n : n + 1024] += v[i * 16 : (i + 1) * 16]

        @pl.when(lc == per - 1)
        def _():
            def turn_in(i):
                w = dp[c, i]
                rss[ci, i] = w.astype(jnp.bfloat16)
                gg[f] += jnp.sum(w * pb[c, i].astype(jnp.float32), axis=0, keepdims=True)

            loop(4, turn_in)

            def give(dx):
                xx, dev = owner(dx, cc)
                start(rss.at[ci, xx], rsr.at[rel, me], r_s.at[ci, dx], r_r.at[rel, me], dev)

            def give_loss(dx):
                xx, dev = owner(dx, cc)
                start(lr.at[ci, xx], lrr.at[rel, me], q_s.at[ci, dx], q_r.at[rel, me], dev)

            loop(3, lambda i: give(i + 1))
            pl.when(ci >= 2)(lambda: give(0))
            loop(3, lambda i: arrived(lr.at[ci, ydev(i + 1)], l_r.at[ci, ydev(i + 1)]))
            loop(3, lambda i: give_loss(i + 1))
            pl.when(ci >= 2)(lambda: give_loss(0))

    def gather_sum(rel):
        out_acc[...] = dp[rel * 2 + core, x]
        accl[...] = lr[rel, x]

        def add(i):
            src = lax.rem(me + 1 + i, 8)
            arrived(rsr.at[rel, src], r_r.at[rel, src])
            out_acc[...] += rsr[rel, src].astype(jnp.float32)
            arrived(lrr.at[rel, src], q_r.at[rel, src])
            accl[...] += lrr[rel, src]

        loop(7, add)

    def stage(t, lag, fn):
        pl.when(jnp.logical_and(t >= lag, t < S + lag))(lambda: fn(t - lag))

    def tick(t):
        @pl.when(t == per)
        def _():
            hand_on(2 + core, 12)

        pl.when(t < S)(lambda: stage_m1(t))

        @pl.when(t == per - 1)
        def _():
            arrived(pb.at[2 + core, x], ag_r.at[2 + core, x])
            spread(2 + core, 8)

        stage(t, EDGE, stage_edge)
        stage(t, CROSS, stage_cross)
        stage(t, BACK, stage_back)
        stage(t, EW, stage_ew)
        stage(t, M2, stage_m2)

        @pl.when(t == S - 2 + M2)
        def _():
            gather_sum(1)
            cb[...] = out_acc[...].astype(jnp.bfloat16)
            clb[...] = accl[...]
            start(cb, cr, c_s.at[0], c_r.at[0], other)
            start(clb, clr, c_s.at[1], c_r.at[1], other)

    loop(S + M2, tick)

    loop(15, lambda i: start(gg.at[f], gg.at[f], g_s.at[i + 1], g_r.at[f], {"fsdp": lax.rem(f + 1 + i, 16)}))
    gather_sum(0)
    arrived(cr, c_r.at[0])
    arrived(clr, c_r.at[1])
    out_acc[...] = (out_acc[...] + cr[...].astype(jnp.float32)) * 0.25
    out_loss[...] = (accl[...] + clr[...]) * (1.0 / (LC * per * 16))
    out_gain[...] = gg[f]

    def add_gain(i):
        src = lax.rem(f + 1 + i, 16)
        arrived(gg.at[src], g_r.at[src])
        out_gain[...] += gg[src]

    loop(15, add_gain)
    out_gain[...] = out_gain[...] / gain[...]

    loop(15, lambda i: sent(pb.at[0, 0], ag_s.at[i]))
    loop(15, lambda i: sent(gg.at[f], g_s.at[i + 1]))
    sent(cb, c_s.at[0])
    sent(clb, c_s.at[1])

    def step_left(s):
        for d in (1, 2, 3):
            sent(lg.at[s, 0], y_s.at[s, d])
            sent(db.at[s, 0], b_s.at[s, d])
        sent(es.at[s], z_s.at[s, 0])
        pl.when(inner)(lambda: sent(xs.at[s], z_s.at[s, 1]))

    loop(S, step_left)

    def chunk_left(ci):
        def both(dx):
            sent(rss.at[ci, 0], r_s.at[ci, dx])
            sent(lr.at[ci, 0], q_s.at[ci, dx])

        for d in (1, 2, 3):
            sent(ls.at[ci, 0], l_s.at[ci, d])
            both(d)
        pl.when(ci >= 2)(lambda: both(0))

    loop(4, chunk_left)


def call(K, cid, hidden, gain, head, partner, codes):
    D = hidden.shape[3]
    per = head.shape[2] // LC
    S = 4 * per
    bf, f32 = jnp.bfloat16, jnp.float32
    V, dma = pltpu.VMEM, pltpu.SemaphoreType.DMA
    vmem = pl.BlockSpec(memory_space=pltpu.VMEM)
    scratch = [
        V((16, 16, D), bf), V((256, 16), jnp.int32),
        V((per, D, LC), bf), V((per, LC, D), bf), V((4, 4, 16, D), bf),
        V((S, 4, 16, LC), bf), V((S, 4, 16, LC), bf), V((S, 4, 16, LC), bf),
        V((4, 4, 16, D), f32), V((4, 4, 16, D), bf), V((2, 8, 16, D), bf),
        V((S, K, 16, LC), bf), V((S, 4, 16, LC), bf),
        V((16, D), f32), V((4, 4, 16, 128), f32),
        V((4, 4, 8, 128), f32), V((4, 4, 8, 128), f32), V((2, 8, 8, 128), f32),
        V((16, D), bf), V((16, D), bf), V((8, 128), f32), V((8, 128), f32),
        V((8, 128), f32), V((16, LC), f32), V((16, 1, D), f32),
        V((S, 8, 16, LC), bf), V((S, K, 16, LC), bf),
        pltpu.SMEM((16,), jnp.int32), pltpu.SMEM((8 + K,), jnp.int32),
    ]
    scratch += [
        pltpu.SemaphoreType.REGULAR((3,)), dma, dma((per,)), dma((15,)), dma((4, 4)), dma((S, 4)), dma((S, 4)), dma((S, 2)), dma((S, 2)),
        dma((S, 4)), dma((S, 4)), dma((4, 4)), dma((4, 4)), dma((4, 4)), dma((2, 8)), dma((4, 4)), dma((2, 8)),
        dma((2,)), dma((2,)), dma((16,)), dma((16,)),
    ]
    hbm = pl.BlockSpec(memory_space=pl.ANY)
    return pl.pallas_call(
        functools.partial(kernel, K, per),
        name="distill%d" % K,
        out_shape=(
            jax.ShapeDtypeStruct((16, D), f32),
            jax.ShapeDtypeStruct((8, 128), f32),
            jax.ShapeDtypeStruct((1, D), f32),
            jax.ShapeDtypeStruct((16, 16, 128), f32),
        ),
        in_specs=[pl.BlockSpec(memory_space=pltpu.SMEM), vmem, vmem, hbm, hbm],
        out_specs=(vmem, vmem, vmem, vmem),
        scratch_shapes=scratch,
        compiler_params=pltpu.CompilerParams(
            collective_id=cid, has_side_effects=True, vmem_limit_bytes=60 * 2**20
        ),
    )(partner, gain, codes, hidden, head)


def finish(acc, gain, inv, loss, total, hidden, out_hidden, out_loss, out_gain):
    g = gain[...]

    def note(n):
        dn = acc[n : n + 1, :] * g
        r = inv[n][:, 0:1]
        nm = hidden[0, n].astype(jnp.float32) * r
        mean = jnp.mean(dn * nm, axis=-1, keepdims=True)
        out_hidden[0, n] = (r * (dn - nm * mean)).astype(jnp.bfloat16)

    for n in range(8):
        note(n)

    @pl.when(pl.program_id(0) == 0)
    def _():
        out_loss[...] = loss[0:1, 0:16]
        out_gain[...] = total[...]


def last(acc, gain, inv, loss, total, hidden):
    D = hidden.shape[3]

    def whole(*shape):
        return pl.BlockSpec(shape, lambda i: (0,) * len(shape))

    block = pl.BlockSpec((1, 8, 16, D), lambda i: (0, i, 0, 0))
    return pl.pallas_call(
        finish,
        name="finish",
        grid=(2,),
        out_shape=(
            jax.ShapeDtypeStruct(hidden.shape, jnp.bfloat16),
            jax.ShapeDtypeStruct((1, 16), jnp.float32),
            jax.ShapeDtypeStruct((1, D), jnp.float32),
        ),
        in_specs=[
            pl.BlockSpec((8, D), lambda i: (i, 0)), whole(1, D), pl.BlockSpec((8, 16, 128), lambda i: (i, 0, 0)),
            whole(8, 128), whole(1, D), block,
        ],
        out_specs=(block, whole(1, 16), whole(1, D)),
    )(acc, gain, inv, loss, total, hidden)


def on_device(hidden, gain, head, partner, codes):
    ids = jnp.arange(16, dtype=jnp.int32)
    away = ((ids & 3) < 2) & ((partner & 3) >= 2)
    crossing = jnp.sum(away.astype(jnp.int32))
    args = (hidden, gain, head, partner, codes.T)
    calls = [functools.partial(call, K, i + 1) for i, K in enumerate(SIZES)]
    which = sum((crossing > K).astype(jnp.int32) for K in SIZES[:-1])
    acc, loss, total, inv = lax.switch(which, calls, *args) if len(SIZES) > 1 else calls[0](*args)
    return last(acc, gain, inv, loss, total, hidden)


def solution(mesh):
    return jax.shard_map(
        on_device,
        mesh=mesh,
        in_specs=(P("mp", "fsdp", None, None), P("mp", None), P("mp", None, "fsdp"), P(), P()),
        out_specs=(P("mp", "fsdp", None, None), P("mp", "fsdp"), P("mp", None)),
        check_vma=False,
    )
```

```python
import functools
import math

import jax
import jax.numpy as jnp
from jax import lax
from jax.experimental import pallas as pl
from jax.experimental.pallas import tpu as pltpu
from jax.sharding import PartitionSpec as P

MESH = pl.DeviceIdType.MESH
EPS = 1e-05
LC = 768
ROWS = 16
SIZES = (4, 6, 8)
EDGE, CROSS, BACK, EW, M2 = 2, 4, 6, 8, 10
EARLY, GAP = 1, 0


def kernel(
    K, per, partner, gain, codes, hidden, head,
    out_acc, out_loss, out_gain, inv,
    hs, ct, hv, ht, pb, lg, db, dl, dp, rss, rsr, xs, es, ns, la, ls, lr, lrr,
    cb, cr, clb, clr, accl, tg, gg, za, zc, rank, sel,
    step_on, isem, hsem, ag_s, ag_r, y_s, y_r, z_s, z_r, b_s, b_r, l_s, l_r, r_s, r_r, q_s, q_r, c_s, c_r, g_s, g_r,
):
    S = 4 * per
    mp, f = lax.axis_index("mp"), lax.axis_index("fsdp")
    y, z = mp // 4, lax.rem(mp, 4)
    h, x, core = f // 8, lax.rem(f, 8) // 2, lax.rem(f, 2)
    half = z // 2
    edge = lax.rem(z + 1, 4) < 2
    inner = jnp.logical_not(edge)
    zin, zout = 1 + half, 3 * half
    me = x * 2 + core
    other = {"fsdp": lax.rem(f + 8, 16)}
    sibling = {"fsdp": f + 1 - 2 * core}

    def remote(src, dst, ssem, rsem, dev):
        return pltpu.make_async_remote_copy(src, dst, ssem, rsem, device_id=dev, device_id_type=MESH)

    def start(*copy):
        remote(*copy).start()

    def arrived(dst, rsem):
        remote(dst, dst, rsem, rsem, other).wait_recv()

    def sent(src, ssem):
        remote(src, src, ssem, ssem, other).wait_send()

    def loop(n, body):
        def step(i, _):
            body(i)
            return 0

        lax.fori_loop(0, n, step, 0)

    def chunk(ci):
        return lax.rem((ci + 1) // 2, 2), lax.rem(core + ci // 2, 2)

    first = per + EARLY

    def work(s):
        late = s - EARLY
        mid = jnp.logical_and(s >= first, late < 3 * per)
        ci = jnp.where(s < per, 0, jnp.where(mid, late // per, 3))
        lc = jnp.where(s < per, s, jnp.where(s < first, s - per, jnp.where(mid, lax.rem(late, per), s - 3 * per)))
        return ci, lc

    def ydev(d):
        return lax.rem(y + d, 4)

    def mate(d):
        return {"mp": ydev(d) * 4 + z}

    whole_hidden = pltpu.make_async_copy(hidden.at[0], hs, isem)
    whole_hidden.start()

    def head_part(lc):
        return pltpu.make_async_copy(head.at[0, :, pl.ds(pl.multiple_of(lc * LC, 128), LC)], hv.at[lc], hsem.at[lc])

    loop(per, lambda lc: head_part(lc).start())

    bar = pltpu.get_barrier_semaphore()

    def greet(dev):
        pl.semaphore_signal(bar, inc=1, device_id=dev, device_id_type=MESH)

    loop(3, lambda i: greet({"fsdp": h * 8 + lax.rem(x + i + 1, 4) * 2 + core}))
    greet(sibling)
    loop(3, lambda i: greet(mate(i + 1)))
    up = {"mp": y * 4 + lax.rem(z + 1, 4), "fsdp": jnp.where(z == 3, lax.rem(f + 8, 16), f)}
    greet(up)
    greet({"mp": y * 4 + lax.rem(z + 3, 4), "fsdp": jnp.where(z == 0, lax.rem(f + 8, 16), f)})

    for hh in range(2):
        r = jnp.int32(0)
        for o in range(8):
            m = 4 * (o % 4) + (1 + hh if o < 4 else 3 * hh)
            rank[m] = r
            r = r + (((partner[m] & 3) >> 1) ^ hh)

    def place(p):
        pz, py = p & 3, p >> 2
        return jnp.where(pz == zin, py, jnp.where(pz == zout, 4 + py, 8 + rank[p]))

    def find(j):
        p = partner[4 * j + z]
        sel[j] = jnp.where(edge, jnp.where((p & 3) == z, p >> 2, 4 + j), place(p))
        p = partner[4 * j + zout]
        sel[4 + j] = jnp.where((p & 3) == zout, 0, place(p))

    loop(4, find)

    def pick(j):
        got = jnp.int32(0)
        for o in range(8):
            m = 4 * (o % 4) + (zin if o < 4 else zout)
            away = ((partner[m] & 3) >> 1) != half
            got = jnp.where(jnp.logical_and(away, rank[m] == j), o, got)
        sel[8 + j] = got

    loop(K, pick)

    whole_hidden.wait()

    def pool(n, _):
        states = hs[n].astype(jnp.float32)
        r = lax.rsqrt(jnp.mean(states * states, axis=-1, keepdims=True) + EPS)
        inv[n] = jnp.broadcast_to(r, (16, 128))
        ns[pl.ds(n, 1), :] = jnp.sum(states * r, axis=0, keepdims=True)
        return 0

    lax.fori_loop(0, ROWS, pool, 0, unroll=4)
    pb[core, x] = (ns[...] * gain[...] * 0.25).astype(jnp.bfloat16)

    pl.semaphore_wait(bar, 9)

    def spread(c, i):
        for k, dx in enumerate((1, 3, 2)):
            start(pb.at[c, x], pb.at[c, x], ag_s.at[i + k], ag_r.at[c, x], {"fsdp": h * 8 + lax.rem(x + dx, 4) * 2 + core})
        start(pb.at[c, x], pb.at[c, x], ag_s.at[i + 3], ag_r.at[c, x], sibling)

    def hand_on(c, i):
        for k, dx in enumerate((1, 3, 2)):
            xx = lax.rem(x + dx, 4)
            arrived(pb.at[c, xx], ag_r.at[c, xx])
            start(pb.at[c, xx], pb.at[c, xx], ag_s.at[i + k], ag_r.at[c, xx], sibling)

    def tell(i):
        pl.semaphore_signal(step_on.at[i], inc=1, device_id=up, device_id_type=MESH)

    tell(0)
    spread(core, 1)

    ct[...] = codes[...].T
    la[...] = jnp.zeros_like(la)
    gg[f] = jnp.zeros_like(gg[f])

    def clear(i):
        dp[i // 4, lax.rem(i, 4)] = jnp.zeros(dp.shape[2:], jnp.float32)

    loop(16, clear)

    def turn(lc):
        head_part(lc).wait()

        def part(i):
            r = pl.multiple_of(i * 256, 256)
            ht[lc, :, pl.ds(r, 256)] = hv[lc, pl.ds(r, 256), :].T

        loop(8, part)

    for i in range(3):
        if i < per:
            turn(i)
        pl.semaphore_wait(step_on.at[i], 1)
        if i < 2:
            tell(i + 1)
    start(pb.at[core, x], pb.at[2 + core, x], ag_s.at[0], ag_r.at[2 + core, x], other)
    for i in range(3, per):
        turn(i)
    hand_on(core, 5)

    def stage_m1(s):
        ci, lc = work(s)
        rel, cc = chunk(ci)
        c = rel * 2 + cc

        @pl.when(jnp.logical_and(lc == 0, ci >= 2))
        def _():
            loop(4, lambda i: arrived(pb.at[c, i], ag_r.at[c, i]))

        v = jnp.dot(pb[c].reshape(64, pb.shape[3]), hv[lc], preferred_element_type=jnp.float32).astype(jnp.bfloat16)
        for i in range(4):
            lg[s, i] = v[i * 16 : (i + 1) * 16]
        za[s, y] = lg[s, y]
        for d in (1, 3, 2):
            start(lg.at[s, ydev(d)], za.at[s, y], y_s.at[s, d], y_r.at[s, y], mate(d))

    def outer(s):
        return za.at[s, pl.ds(4, 4)]

    def stage_edge(s):
        loop(3, lambda i: arrived(za.at[s, ydev(i + 1)], y_r.at[s, ydev(i + 1)]))

        @pl.when(edge)
        def _():
            start(za.at[s, pl.ds(0, 4)], outer(s), z_s.at[s, 0], z_r.at[s, 0], {"mp": y * 4 + zin})

    def fetch(s, i, n):
        got = za[s, 0]
        for k in range(1, n):
            got = jnp.where(i == k, za[s, k] if k < 8 else zc[s, k - 8], got)
        return got

    def stage_cross(s):
        @pl.when(inner)
        def _():
            arrived(outer(s), z_r.at[s, 0])

            def put(j):
                xs[s, j] = fetch(s, sel[8 + j], 8)

            loop(K, put)
            start(xs.at[s], zc.at[s], z_s.at[s, 1], z_r.at[s, 1], {"mp": y * 4 + 3 - z})

    def stage_back(s):
        @pl.when(inner)
        def _():
            arrived(zc.at[s], z_r.at[s, 1])

            def put(j):
                es[s, j] = fetch(s, sel[4 + j], 8 + K)

            loop(4, put)
            start(es.at[s], outer(s), z_s.at[s, 0], z_r.at[s, 0], {"mp": y * 4 + zout})

    def stage_ew(s):
        ci, lc = work(s)
        rel, cc = chunk(ci)

        @pl.when(edge)
        def _():
            arrived(outer(s), z_r.at[s, 0])

        hc = jnp.where(rel == 0, h, 1 - h)
        row = pl.multiple_of((hc * 8 + y * 2 + cc) * 16, 16)
        ids = ct[pl.ds(row, 16), :] - (f * (LC * per) + lc * LC)
        lanes = lax.broadcasted_iota(jnp.int32, (16, LC), 1)
        hit = ids[:, 0:1] == lanes
        for j in range(1, 16):
            hit = jnp.logical_or(hit, ids[:, j : j + 1] == lanes)
        tg[...] = jnp.where(hit, 1.0, 0.0)

        def model(j):
            q = fetch(s, sel[j], 8 + K).astype(jnp.float32)
            v = za[s, j].astype(jnp.float32)
            target = tg[...]
            e = jnp.exp(jnp.abs(v) * -0.5)
            e2 = e * e
            a1, b1 = 1.0 + e, 1.0 + e2
            rr = 1.0 / (a1 * b1)
            pos = v >= 0.0
            s12 = (jnp.where(pos, 1.0, e2) * a1 + jnp.where(pos, 1.0, e) * b1) * rr
            eq = jnp.exp(jnp.abs(q) * -0.5)
            t = jnp.where(q >= 0.0, 1.0, eq) / (1.0 + eq)
            db[s, j] = (s12 - target - t).astype(jnp.bfloat16)
            each = 2.0 * jnp.maximum(v, 0.0) + jnp.log(a1 * a1 * b1) - (t + target) * v
            part = each[:, 0:128]
            for k in range(128, LC, 128):
                part = part + each[:, k : k + 128]
            la[ci, j] += part

        loop(4, model)
        dl[s, y] = db[s, y]
        for d in (1, 3, 2):
            start(db.at[s, ydev(d)], dl.at[s, y], b_s.at[s, d], b_r.at[s, y], mate(d))

        @pl.when(lc == per - 1)
        def _():
            diag = lax.broadcasted_iota(jnp.int32, (16, 128), 0) == lax.broadcasted_iota(jnp.int32, (16, 128), 1)

            def line(j):
                total = jnp.sum(la[ci, j], axis=1, keepdims=True)
                row = jnp.sum(jnp.where(diag, total, 0.0), axis=0, keepdims=True)
                ls[ci, j] = jnp.broadcast_to(row, (8, 128))

            loop(4, line)
            lr[ci, y] = ls[ci, y]
            for d in (1, 3, 2):
                start(ls.at[ci, ydev(d)], lr.at[ci, y], l_s.at[ci, d], l_r.at[ci, y], mate(d))

    def owner(dx, cc):
        xx = lax.rem(x + dx, 4)
        return xx, {"fsdp": h * 8 + xx * 2 + cc}

    def stage_m2(s):
        ci, lc = work(s)
        rel, cc = chunk(ci)
        c = rel * 2 + cc
        loop(3, lambda i: arrived(dl.at[s, ydev(i + 1)], b_r.at[s, ydev(i + 1)]))
        left = dl[s].reshape(64, LC)
        for n in range(0, 2048, 1024):
            v = jnp.dot(left, ht[lc, :, n : n + 1024], preferred_element_type=jnp.float32)
            for i in range(4):
                dp[c, i, :, n : n + 1024] += v[i * 16 : (i + 1) * 16]

        @pl.when(lc == per - 1)
        def _():
            def turn_in(i):
                w = dp[c, i]
                rss[ci, i] = w.astype(jnp.bfloat16)
                gg[f] += jnp.sum(w * pb[c, i].astype(jnp.float32), axis=0, keepdims=True)

            loop(4, turn_in)

            def give(dx):
                xx, dev = owner(dx, cc)
                start(rss.at[ci, xx], rsr.at[rel, me], r_s.at[ci, dx], r_r.at[rel, me], dev)

            def give_loss(dx):
                xx, dev = owner(dx, cc)
                start(lr.at[ci, xx], lrr.at[rel, me], q_s.at[ci, dx], q_r.at[rel, me], dev)

            loop(3, lambda i: give(i + 1))
            pl.when(ci >= 2)(lambda: give(0))
            loop(3, lambda i: arrived(lr.at[ci, ydev(i + 1)], l_r.at[ci, ydev(i + 1)]))
            loop(3, lambda i: give_loss(i + 1))
            pl.when(ci >= 2)(lambda: give_loss(0))

    def gather_sum(rel):
        out_acc[...] = dp[rel * 2 + core, x]
        accl[...] = lr[rel, x]

        def add(i):
            src = lax.rem(me + 1 + i, 8)
            arrived(rsr.at[rel, src], r_r.at[rel, src])
            out_acc[...] += rsr[rel, src].astype(jnp.float32)
            arrived(lrr.at[rel, src], q_r.at[rel, src])
            accl[...] += lrr[rel, src]

        loop(7, add)

    def stage(t, lag, fn):
        u = t - lag
        late = u >= first + GAP
        on = jnp.logical_and(u >= 0, jnp.logical_or(u < first, late))
        s = jnp.where(late, u - GAP, u)
        pl.when(jnp.logical_and(on, s < S))(lambda: fn(s))

    def tick(t):
        @pl.when(t == first + GAP)
        def _():
            hand_on(2 + core, 12)

        stage(t, 0, stage_m1)
        stage(t, EDGE, stage_edge)
        stage(t, CROSS, stage_cross)

        @pl.when(t == first + max(GAP - 3, -1))
        def _():
            arrived(pb.at[2 + core, x], ag_r.at[2 + core, x])
            spread(2 + core, 8)

        stage(t, BACK, stage_back)
        stage(t, EW, stage_ew)
        stage(t, M2, stage_m2)

    loop(S + GAP + M2, tick)

    loop(15, lambda i: start(gg.at[f], gg.at[f], g_s.at[i + 1], g_r.at[f], {"fsdp": lax.rem(f + 1 + i, 16)}))
    gather_sum(1)
    cb[...] = out_acc[...].astype(jnp.bfloat16)
    clb[...] = accl[...]
    start(cb, cr, c_s.at[0], c_r.at[0], other)
    start(clb, clr, c_s.at[1], c_r.at[1], other)
    gather_sum(0)
    arrived(cr, c_r.at[0])
    arrived(clr, c_r.at[1])
    out_acc[...] = (out_acc[...] + cr[...].astype(jnp.float32)) * 0.25
    out_loss[...] = (accl[...] + clr[...]) * (1.0 / (LC * per * 16))
    out_gain[...] = gg[f]

    def add_gain(i):
        src = lax.rem(f + 1 + i, 16)
        arrived(gg.at[src], g_r.at[src])
        out_gain[...] += gg[src]

    loop(15, add_gain)
    out_gain[...] = out_gain[...] / gain[...]

    loop(15, lambda i: sent(pb.at[0, 0], ag_s.at[i]))
    loop(15, lambda i: sent(gg.at[f], g_s.at[i + 1]))
    sent(cb, c_s.at[0])
    sent(clb, c_s.at[1])

    def step_left(s):
        for d in (1, 2, 3):
            sent(lg.at[s, 0], y_s.at[s, d])
            sent(db.at[s, 0], b_s.at[s, d])
        sent(es.at[s], z_s.at[s, 0])
        pl.when(inner)(lambda: sent(xs.at[s], z_s.at[s, 1]))

    loop(S, step_left)

    def chunk_left(ci):
        def both(dx):
            sent(rss.at[ci, 0], r_s.at[ci, dx])
            sent(lr.at[ci, 0], q_s.at[ci, dx])

        for d in (1, 2, 3):
            sent(ls.at[ci, 0], l_s.at[ci, d])
            both(d)
        pl.when(ci >= 2)(lambda: both(0))

    loop(4, chunk_left)


def call(K, cid, hidden, gain, head, partner, codes):
    D = hidden.shape[3]
    per = head.shape[2] // LC
    S = 4 * per
    bf, f32 = jnp.bfloat16, jnp.float32
    V, dma = pltpu.VMEM, pltpu.SemaphoreType.DMA
    vmem = pl.BlockSpec(memory_space=pltpu.VMEM)
    scratch = [
        V((16, 16, D), bf), V((256, 16), jnp.int32),
        V((per, D, LC), bf), V((per, LC, D), bf), V((4, 4, 16, D), bf),
        V((S, 4, 16, LC), bf), V((S, 4, 16, LC), bf), V((S, 4, 16, LC), bf),
        V((4, 4, 16, D), f32), V((4, 4, 16, D), bf), V((2, 8, 16, D), bf),
        V((S, K, 16, LC), bf), V((S, 4, 16, LC), bf),
        V((16, D), f32), V((4, 4, 16, 128), f32),
        V((4, 4, 8, 128), f32), V((4, 4, 8, 128), f32), V((2, 8, 8, 128), f32),
        V((16, D), bf), V((16, D), bf), V((8, 128), f32), V((8, 128), f32),
        V((8, 128), f32), V((16, LC), f32), V((16, 1, D), f32),
        V((S, 8, 16, LC), bf), V((S, K, 16, LC), bf),
        pltpu.SMEM((16,), jnp.int32), pltpu.SMEM((8 + K,), jnp.int32),
    ]
    scratch += [
        pltpu.SemaphoreType.REGULAR((3,)), dma, dma((per,)), dma((15,)), dma((4, 4)), dma((S, 4)), dma((S, 4)), dma((S, 2)), dma((S, 2)),
        dma((S, 4)), dma((S, 4)), dma((4, 4)), dma((4, 4)), dma((4, 4)), dma((2, 8)), dma((4, 4)), dma((2, 8)),
        dma((2,)), dma((2,)), dma((16,)), dma((16,)),
    ]
    hbm = pl.BlockSpec(memory_space=pl.ANY)
    return pl.pallas_call(
        functools.partial(kernel, K, per),
        name="distill%d" % K,
        out_shape=(
            jax.ShapeDtypeStruct((16, D), f32),
            jax.ShapeDtypeStruct((8, 128), f32),
            jax.ShapeDtypeStruct((1, D), f32),
            jax.ShapeDtypeStruct((16, 16, 128), f32),
        ),
        in_specs=[pl.BlockSpec(memory_space=pltpu.SMEM), vmem, vmem, hbm, hbm],
        out_specs=(vmem, vmem, vmem, vmem),
        scratch_shapes=scratch,
        compiler_params=pltpu.CompilerParams(
            collective_id=cid, has_side_effects=True, vmem_limit_bytes=60 * 2**20
        ),
    )(partner, gain, codes, hidden, head)


def finish(acc, gain, inv, loss, total, hidden, out_hidden, out_loss, out_gain):
    g = gain[...]

    def note(n):
        dn = acc[n : n + 1, :] * g
        r = inv[n][:, 0:1]
        nm = hidden[0, n].astype(jnp.float32) * r
        mean = jnp.mean(dn * nm, axis=-1, keepdims=True)
        out_hidden[0, n] = (r * (dn - nm * mean)).astype(jnp.bfloat16)

    for n in range(8):
        note(n)

    @pl.when(pl.program_id(0) == 0)
    def _():
        out_loss[...] = loss[0:1, 0:16]
        out_gain[...] = total[...]


def last(acc, gain, inv, loss, total, hidden):
    D = hidden.shape[3]

    def whole(*shape):
        return pl.BlockSpec(shape, lambda i: (0,) * len(shape))

    block = pl.BlockSpec((1, 8, 16, D), lambda i: (0, i, 0, 0))
    return pl.pallas_call(
        finish,
        name="finish",
        grid=(2,),
        out_shape=(
            jax.ShapeDtypeStruct(hidden.shape, jnp.bfloat16),
            jax.ShapeDtypeStruct((1, 16), jnp.float32),
            jax.ShapeDtypeStruct((1, D), jnp.float32),
        ),
        in_specs=[
            pl.BlockSpec((8, D), lambda i: (i, 0)), whole(1, D), pl.BlockSpec((8, 16, 128), lambda i: (i, 0, 0)),
            whole(8, 128), whole(1, D), block,
        ],
        out_specs=(block, whole(1, 16), whole(1, D)),
    )(acc, gain, inv, loss, total, hidden)


def on_device(hidden, gain, head, partner, codes):
    ids = jnp.arange(16, dtype=jnp.int32)
    away = ((ids & 3) < 2) & ((partner & 3) >= 2)
    crossing = jnp.sum(away.astype(jnp.int32))
    args = (hidden, gain, head, partner, codes.T)
    k0, k1, k2 = [functools.partial(call, K, i + 1) for i, K in enumerate(SIZES)]

    def more(*args):
        return lax.cond(crossing > SIZES[1], k2, k1, *args)

    acc, loss, total, inv = lax.cond(crossing > SIZES[0], more, k0, *args)
    return last(acc, gain, inv, loss, total, hidden)


def solution(mesh):
    return jax.shard_map(
        on_device,
        mesh=mesh,
        in_specs=(P("mp", "fsdp", None, None), P("mp", None), P("mp", None, "fsdp"), P(), P()),
        out_specs=(P("mp", "fsdp", None, None), P("mp", "fsdp"), P("mp", None)),
        check_vma=False,
    )
```
